256 devices in a mesh: gx: 16 (over y_hi, z), gy: 16 (over y_lo, x, core).
Axes of the slice: x: 4, y: 4 (y_hi: 2, y_lo: 2; y = y_hi * 2 + y_lo), z: 8, core: 2. Of those that a mesh axis runs over, the one named last changes fastest.
Arguments:
- cotangent: bfloat16 [32, 3072, 4096], P(None, 'gx', 'gy'), may hold values from -6 to 6
- preact: bfloat16 [32, 3072, 4096], P(None, 'gx', 'gy'), may hold values from -6 to 6
- spectrum: float32 [16384, 2, 32], P(('gx', 'gy')), may hold values from -0.5 to 0.5
- spectral_weight: float32 [16384, 2, 1024], P(('gx', 'gy')), may hold values from -1 to 1
- point_weight: float32 [32, 32], replicated, may hold values from -1 to 1
Outputs:
- input_grad: bfloat16 [32, 3072, 4096], P(None, 'gx', 'gy')
- weight_grad: float32 [16384, 2, 1024], P(('gx', 'gy'))
The draws below stay inside these ranges and needn't reach their ends.
All inputs are finite; a program needn't handle non-finite values.
Results may differ from the reference program's by a relative error of at most 0.0011.
Values sent between devices are 32-bit elements; how exact they have to be, the bound alone decides.
No kernel may reach another device: no remote copies, remote signals or barrier semaphores. Data moves between devices by JAX's collectives and lax.ppermute only.
A program may use at most 128 MiB of HBM per device.

```python
import math
import jax
import jax.numpy as jnp
from jax import lax

C = 32
K1 = 128
K2 = 128
NX = 3072
NY = 4096
MODES = 16384


def levels(rng, dims, cuts, low, high):
    def one(dim, blocks):
        steps = jax.random.uniform(jax.random.fold_in(jax.random.fold_in(rng, 6), dim), (blocks,), jnp.float32, low / len(cuts), high / len(cuts))
        return jnp.repeat(jnp.exp(steps), dims[dim] // blocks).reshape((-1,) + (1,) * (len(dims) - dim - 1))

    gain = one(*cuts[0])
    for cut in cuts[1:]:
        gain = gain * one(*cut)
    return gain


def gaussian(rng, dims, spread, most, shards=(), kind=jnp.bfloat16):
    values = spread * jax.random.normal(rng, dims, jnp.float32)
    if shards:
        values = values * levels(rng, dims, shards, -0.22, 0.18)
    return jnp.clip(values, -most, most).astype(kind)


def setup_inputs(seed: int = 0) -> dict:
    seeds = jax.random.split(jax.random.key(seed), 6)
    return {
        "cotangent": gaussian(seeds[0], (C, NX, NY), 1.0, 6.0, ((1, 16), (2, 16))),
        "preact": gaussian(seeds[1], (C, NX, NY), 1.0, 6.0, ((1, 16), (2, 16))),
        "spectrum": gaussian(seeds[2], (MODES, 2, C), 0.0625, 0.5, ((0, 256),), jnp.float32),
        "spectral_weight": gaussian(seeds[3], (MODES, 2, C * C), C ** -0.5, 1.0, ((0, 256),), jnp.float32),
        "point_weight": gaussian(seeds[4], (C, C), C ** -0.5, 1.0, (), jnp.float32),
    }


highest = lax.Precision.HIGHEST

def gelu_slope(values):
    cumul = 0.5 * (1.0 + jax.scipy.special.erf(values * 0.7071067811865476))
    return cumul + values * jnp.exp(-0.5 * values * values) * 0.3989422804014327

def mode_work(mode_grad, spectrum, spectral_weight):
    mode_count = mode_grad.shape[0]
    chans = mode_grad.shape[2]
    weights = spectral_weight.reshape(mode_count, 2, chans, chans)
    weight_real, weight_imag = (weights[:, 0], weights[:, 1])
    grad_real, grad_imag = (mode_grad[:, 0], mode_grad[:, 1])
    saved_real, saved_imag = (spectrum[:, 0], spectrum[:, 1])
    out_real = saved_real[:, :, None] * grad_real[:, None, :] + saved_imag[:, :, None] * grad_imag[:, None, :]
    out_imag = saved_real[:, :, None] * grad_imag[:, None, :] - saved_imag[:, :, None] * grad_real[:, None, :]
    weight_grad = jnp.stack([out_real, out_imag], axis=1).reshape(mode_count, 2, chans * chans)
    back_real = lax.optimization_barrier(jnp.sum(weight_real * grad_real[:, None, :] + weight_imag * grad_imag[:, None, :], axis=-1))
    back_imag = lax.optimization_barrier(jnp.sum(weight_real * grad_imag[:, None, :] - weight_imag * grad_real[:, None, :], axis=-1))
    return (weight_grad, back_real, back_imag)

def reference(cotangent, preact, spectrum, spectral_weight, point_weight):
    upstream = cotangent.astype(jnp.float32) * gelu_slope(preact.astype(jnp.float32))
    wave_rows = jnp.arange(K1, dtype=jnp.int32)
    row_index = jnp.where(wave_rows < K1 // 2, wave_rows, NX - K1 + wave_rows).astype(jnp.int32)
    column_index = jnp.arange(K2, dtype=jnp.int32)

    def forward_one(channel):
        spectra = jnp.fft.fft2(channel)
        picked = spectra[row_index][:, column_index]
        return jnp.stack([jnp.real(picked), jnp.imag(picked)])
    hats = lax.map(forward_one, upstream)
    mode_grad = jnp.transpose(hats, (2, 3, 1, 0)).reshape(MODES, 2, C) * (1.0 / math.sqrt(K1 * K2))
    weight_grad, back_real, back_imag = mode_work(mode_grad, spectrum, spectral_weight)
    grid_real = jnp.transpose(back_real.reshape(K1, K2, C), (2, 0, 1))
    grid_imag = jnp.transpose(back_imag.reshape(K1, K2, C), (2, 0, 1))

    def inverse_one(packed):
        part_real, part_imag, weight_row = packed
        zeros_field = jnp.zeros((NX, NY), jnp.float32)
        field = lax.complex(zeros_field, zeros_field)
        field = field.at[row_index[:, None], column_index[None, :]].set(lax.complex(part_real, part_imag))
        spatial = jnp.real(jnp.fft.ifft2(field)) * (NX * NY / math.sqrt(NX * NY))
        local = jnp.tensordot(weight_row, upstream, axes=1, precision=highest)
        return (spatial + local).astype(jnp.bfloat16)
    input_grad = lax.map(inverse_one, (grid_real, grid_imag, point_weight))
    return (input_grad, weight_grad)
```

```python
import math

import jax
import jax.numpy as jnp
import numpy as np
from jax import lax
from jax.sharding import PartitionSpec as P

K1 = 128
K2 = 128
ROW_RANK = 20
COL_RANK = 28

highest = lax.Precision.HIGHEST


def slepian(length, half_band, count):
    place = np.arange(length)
    main = ((length - 1 - 2 * place) / 2.0) ** 2 * math.cos(2.0 * math.pi * half_band)
    side = place[1:] * (length - place[1:]) / 2.0
    _, vectors = np.linalg.eigh(np.diag(main) + np.diag(side, 1) + np.diag(side, -1))
    basis = vectors[:, ::-1][:, :count]
    tilt = 1.0 + (place - (length - 1) / 2.0) / length
    return basis * np.sign(np.sum(basis * tilt[:, None], axis=0))


def band_tables(freqs, half_band, grid, blocks, count):
    here = grid // blocks
    basis = slepian(here, half_band, count)
    turns = freqs[:, None] * np.arange(grid)[None, :] % grid
    waves = np.exp(-2j * math.pi * turns / grid).reshape(len(freqs), blocks, here)
    return basis, np.einsum("fbp,pn->bfn", waves, basis)


def gelu_slope(values):
    cumul = 0.5 * (1.0 + jax.scipy.special.erf(values * 0.7071067811865476))
    return cumul + values * jnp.exp(-0.5 * values * values) * 0.3989422804014327


def mode_work(mode_grad, spectrum, spectral_weight):
    mode_count = mode_grad.shape[0]
    chans = mode_grad.shape[2]
    weights = spectral_weight.reshape(mode_count, 2, chans, chans)
    weight_real, weight_imag = (weights[:, 0], weights[:, 1])
    grad_real, grad_imag = (mode_grad[:, 0], mode_grad[:, 1])
    saved_real, saved_imag = (spectrum[:, 0], spectrum[:, 1])
    out_real = (
        saved_real[:, :, None] * grad_real[:, None, :]
        + saved_imag[:, :, None] * grad_imag[:, None, :]
    )
    out_imag = (
        saved_real[:, :, None] * grad_imag[:, None, :]
        - saved_imag[:, :, None] * grad_real[:, None, :]
    )
    weight_grad = jnp.stack([out_real, out_imag], axis=1).reshape(mode_count, 2, chans * chans)
    back_real = jnp.sum(
        weight_real * grad_real[:, None, :] + weight_imag * grad_imag[:, None, :], axis=-1
    )
    back_imag = jnp.sum(
        weight_real * grad_imag[:, None, :] - weight_imag * grad_real[:, None, :], axis=-1
    )
    return (weight_grad, jnp.stack([back_real, back_imag], axis=1))


def on_device(cotangent, preact, spectrum, spectral_weight, point_weight):
    chans, rows_here, cols_here = cotangent.shape
    gx, gy = lax.axis_size("gx"), lax.axis_size("gy")
    grid_rows, grid_cols = rows_here * gx, cols_here * gy
    share = chans // gy
    half = K1 * K2 // (gx * gy)
    wave_rows = np.arange(K1)
    row_freqs = np.where(wave_rows < K1 // 2, wave_rows, wave_rows - K1)
    row_basis, row_waves = band_tables(row_freqs, K1 / 2 / grid_rows, grid_rows, gx, ROW_RANK)
    col_basis, col_waves = band_tables(
        np.arange(K2), (K2 - 1) / grid_cols, grid_cols, gy, COL_RANK
    )
    row_basis = jnp.asarray(row_basis, jnp.float32)
    col_basis = jnp.asarray(col_basis, jnp.float32)
    row_waves = jnp.asarray(np.stack([row_waves.real, row_waves.imag], 1), jnp.float32)
    col_waves = jnp.asarray(np.stack([col_waves.real, col_waves.imag], 1), jnp.float32)
    mine = row_waves[lax.axis_index("gx")]

    upstream = cotangent.astype(jnp.float32) * gelu_slope(preact.astype(jnp.float32))
    pointwise = jnp.einsum("io,oxy->ixy", point_weight, upstream, precision=lax.Precision.HIGH)
    narrow = jnp.einsum("cxy,yb->cxb", upstream, col_basis, precision=lax.Precision.HIGH)
    small = jnp.einsum("cxb,xa->cab", narrow, row_basis, precision=highest)

    blocks = lax.all_to_all(
        small.reshape(gy, share, ROW_RANK, COL_RANK), "gy", 0, 0
    )
    wide = jnp.einsum("gcab,gqjb->qcaj", blocks, col_waves, precision=highest)
    real = jnp.einsum("ka,caj->kcj", mine[0], wide[0], precision=highest) - jnp.einsum(
        "ka,caj->kcj", mine[1], wide[1], precision=highest
    )
    imag = jnp.einsum("ka,caj->kcj", mine[0], wide[1], precision=highest) + jnp.einsum(
        "ka,caj->kcj", mine[1], wide[0], precision=highest
    )
    terms = jnp.stack([real, imag], axis=1)
    terms = terms.reshape(K1, 2, share, K2 // half, half).transpose(0, 3, 1, 2, 4)
    terms = terms.reshape(gx * gy, 2, share * half)
    got = lax.all_to_all(terms, ("gx", "gy"), 0, 0)
    got = jnp.sum(got.reshape(gx, gy, 2, share, half), axis=0)
    mode_grad = got.transpose(3, 1, 0, 2).reshape(half, 2, chans) * (1.0 / math.sqrt(K1 * K2))

    weight_grad, spectrum_grad = mode_work(mode_grad, spectrum, spectral_weight)

    back = spectrum_grad.reshape(half, 2, gy, share).transpose(2, 1, 3, 0)
    back = back.reshape(1, gy, 2, share * half)
    back = jnp.broadcast_to(back, (gx, gy, 2, share * half)).reshape(gx * gy, 2, share * half)
    modes = lax.all_to_all(back, ("gx", "gy"), 0, 0)
    modes = modes.reshape(K1, K2 // half, 2, share, half).transpose(2, 0, 3, 1, 4)
    modes = modes.reshape(2, K1, share, K2)
    real = jnp.einsum("ka,kcj->caj", mine[0], modes[0], precision=highest) + jnp.einsum(
        "ka,kcj->caj", mine[1], modes[1], precision=highest
    )
    imag = jnp.einsum("ka,kcj->caj", mine[0], modes[1], precision=highest) - jnp.einsum(
        "ka,kcj->caj", mine[1], modes[0], precision=highest
    )
    spread = jnp.einsum("qcaj,gqjb->gcab", jnp.stack([real, imag]), col_waves, precision=highest)
    small = lax.all_to_all(spread, "gy", 0, 0).reshape(chans, ROW_RANK, COL_RANK)
    small = small * (1.0 / math.sqrt(grid_rows * grid_cols))
    narrow = jnp.einsum("cab,xa->cxb", small, row_basis, precision=highest)
    spectral = jnp.einsum("cxb,yb->cxy", narrow, col_basis, precision=lax.Precision.HIGH)
    return ((spectral + pointwise).astype(jnp.bfloat16), weight_grad)


def solution(mesh):
    placed = (
        P(None, "gx", "gy"),
        P(None, "gx", "gy"),
        P(("gx", "gy"), None, None),
        P(("gx", "gy"), None, None),
        P(),
    )
    return jax.shard_map(
        on_device,
        mesh=mesh,
        in_specs=placed,
        out_specs=(P(None, "gx", "gy"), P(("gx", "gy"), None, None)),
        check_vma=False,
    )
```

```python
import functools
import math

import jax
import jax.numpy as jnp
import ml_dtypes
import numpy as np
from jax import lax
from jax.experimental import pallas as pl
from jax.experimental.pallas import tpu as pltpu
from jax.sharding import PartitionSpec as P

K1 = 128
K2 = 128
RANK = 32
PART = 16
LANES = 128
FOLD = 4
ROWS = 32

F32 = jnp.float32
BF16 = jnp.bfloat16


def slepian(length, half_band, count):
    place = np.arange(length)
    main = ((length - 1 - 2 * place) / 2.0) ** 2 * math.cos(2.0 * math.pi * half_band)
    side = place[1:] * (length - place[1:]) / 2.0
    _, vectors = np.linalg.eigh(np.diag(main) + np.diag(side, 1) + np.diag(side, -1))
    basis = vectors[:, ::-1][:, :count]
    tilt = 1.0 + (place - (length - 1) / 2.0) / length
    return basis * np.sign(np.sum(basis * tilt[:, None], axis=0))


def band_tables(freqs, half_band, grid, blocks):
    here = grid // blocks
    basis = slepian(here, half_band, RANK)
    turns = freqs[:, None] * np.arange(grid)[None, :] % grid
    waves = np.exp(-2j * math.pi * turns / grid).reshape(len(freqs), blocks, here)
    return basis, np.einsum("fbp,pn->bfn", waves, basis)


def halves(table):
    table = np.asarray(table, np.float32)
    high = table.astype(ml_dtypes.bfloat16)
    return high, (table - high.astype(np.float32)).astype(ml_dtypes.bfloat16)


def split(values):
    high = values.astype(BF16)
    return high, (values - high.astype(F32)).astype(BF16)


def dot(left, right):
    return jnp.dot(left, right, preferred_element_type=F32)


def dot3(left, right):
    return dot(left[0], right[0]) + (dot(left[0], right[1]) + dot(left[1], right[0]))


def gelu_slope(values):
    cumul = 0.5 * (1.0 + lax.erf(values * 0.7071067811865476))
    return cumul + values * jnp.exp(-0.5 * values * values) * 0.3989422804014327


def lane_group(rows):
    return lax.broadcasted_iota(jnp.int32, (rows, LANES), 1) // RANK


def low_lanes(rows):
    return lax.broadcasted_iota(jnp.int32, (rows, LANES), 1) < LANES // 2


def swap_lanes(values):
    return pltpu.roll(values, LANES // 2, 1)


def turn_blocks(pieces):
    group = lane_group(pieces[0].shape[0])
    out = []
    for t in range(FOLD):
        total = None
        for s in range(FOLD):
            shift = (s - t) * RANK % LANES
            moved = pltpu.roll(pieces[s], shift, 1) if shift else pieces[s]
            total = moved if total is None else jnp.where(group == s, moved, total)
        out.append(total)
    return out


def project_kernel(cot_ref, pre_ref, col_ref, row_hi_ref, row_lo_ref, out_ref, held):
    step = pl.program_id(0)
    count = 8 * 16
    group = lane_group(count)
    col = col_ref[...]
    for part in range(ROWS // 16):
        rows = pl.ds(part * 16, 16)
        total = None
        for q in range(FOLD):
            chans = pl.ds(q * 8, 8)
            grad = cot_ref[chans, rows, :].astype(F32)
            upstream = grad * gelu_slope(pre_ref[chans, rows, :].astype(F32))
            high, low = split(upstream.reshape(count, upstream.shape[2]))
            both = dot(high, col)
            narrow = both[:, :LANES] + (both[:, LANES:] + dot(low, col[:, :LANES]))
            total = narrow if total is None else jnp.where(group == q, narrow, total)
        place = pl.multiple_of(step * ROWS + part * 16, 16)
        held[:, pl.ds(place, 16), :] = total.reshape(8, 16, LANES)

    @pl.when(step == pl.num_programs(0) - 1)
    def _():
        row = (row_hi_ref[...], row_lo_ref[...])
        low = low_lanes(PART)
        for g in range(8):
            small = dot3(row, split(held[g]))
            first, second = small[:PART], small[PART:]
            out_ref[2 * g] = jnp.where(low, first, swap_lanes(second))
            out_ref[2 * g + 1] = jnp.where(low, swap_lanes(first), second)


def project(cotangent, preact, row_basis, col_basis):
    chans, rows, cols = cotangent.shape
    col_hi, col_lo = halves(np.tile(col_basis, (1, FOLD)))
    col = np.concatenate([col_hi, col_lo], 1)
    row_hi, row_lo = halves(row_basis.T)
    grid_spec = pl.BlockSpec((chans, ROWS, cols), lambda s: (0, s, 0))
    whole = lambda shape: pl.BlockSpec(shape, lambda s: (0,) * len(shape))
    return pl.pallas_call(
        project_kernel,
        grid=(rows // ROWS,),
        in_specs=[grid_spec, grid_spec, whole(col.shape), whole(row_hi.shape), whole(row_lo.shape)],
        out_specs=whole((16, PART, LANES)),
        out_shape=jax.ShapeDtypeStruct((16, PART, LANES), F32),
        scratch_shapes=[pltpu.VMEM((8, rows, LANES), F32)],
        compiler_params=pltpu.CompilerParams(vmem_limit_bytes=32 * 2**20),
        name="project",
    )(cotangent, preact, jnp.asarray(col), jnp.asarray(row_hi), jnp.asarray(row_lo))


def waves_kernel(blocks_ref, col_hi_ref, col_lo_ref, row_hi_ref, row_lo_ref, out_ref):
    strips = [turn_blocks([blocks_ref[4 * s + t] for t in range(FOLD)]) for s in range(4)]
    small = jnp.concatenate(
        [jnp.concatenate([strips[s][t] for s in range(4)], 1) for t in range(FOLD)], 0
    )
    wide = dot3(split(small), (col_hi_ref[...], col_lo_ref[...]))
    low = low_lanes(PART)
    row = (row_hi_ref[...], row_lo_ref[...])
    for half in range(2):
        tall = []
        for ri in range(2):
            for ah in range(2):
                first = wide[(2 * ah) * PART : (2 * ah + 1) * PART, ri * LANES : (ri + 1) * LANES]
                second = wide[(2 * ah + 1) * PART : (2 * ah + 2) * PART, ri * LANES : (ri + 1) * LANES]
                if half == 0:
                    tall.append(jnp.where(low, first, swap_lanes(second)))
                else:
                    tall.append(jnp.where(low, swap_lanes(first), second))
        terms = dot3(row, split(jnp.concatenate(tall, 0)))
        out_ref[:, half, 0, :] = terms[:K1]
        out_ref[:, half, 1, :] = terms[K1:]


def to_waves(blocks, col, row):
    return pl.pallas_call(
        waves_kernel,
        out_shape=jax.ShapeDtypeStruct((K1, 2, 2, LANES), F32),
        name="to_waves",
    )(blocks, *col, *row)


def blocks_kernel(modes_ref, col_hi_ref, col_lo_ref, row_hi_ref, row_lo_ref, out_ref):
    row = (row_hi_ref[...], row_lo_ref[...])
    tall = []
    for half in range(2):
        modes = jnp.concatenate([modes_ref[:, half, 0, :], modes_ref[:, half, 1, :]], 0)
        tall.append(dot3(row, split(modes)))
    low = low_lanes(PART)
    rows = []
    for ah in range(2):
        for q in range(2):
            cells = []
            for ri in range(2):
                place = slice(ri * RANK + ah * PART, ri * RANK + (ah + 1) * PART)
                first, second = tall[0][place], tall[1][place]
                if q == 0:
                    cells.append(jnp.where(low, first, swap_lanes(second)))
                else:
                    cells.append(jnp.where(low, swap_lanes(first), second))
            rows.append(jnp.concatenate(cells, 1))
    small = dot3(split(jnp.concatenate(rows, 0)), (col_hi_ref[...], col_lo_ref[...]))
    for s in range(4):
        pieces = turn_blocks(
            [small[t * PART : (t + 1) * PART, s * LANES : (s + 1) * LANES] for t in range(FOLD)]
        )
        for t in range(FOLD):
            out_ref[4 * s + t] = pieces[t]


def to_blocks(modes, col, row):
    return pl.pallas_call(
        blocks_kernel,
        out_shape=jax.ShapeDtypeStruct((16, PART, LANES), F32),
        name="to_blocks",
    )(modes, *col, *row)


def expand_kernel(blocks_ref, local_ref, col_ref, row_ref, out_ref, held):
    step = pl.program_id(0)

    @pl.when(step == 0)
    def _():
        group = lane_group(PART)
        col = col_ref[...]
        for d in range(16):
            block = blocks_ref[d]
            masked = jnp.concatenate([jnp.where(group == t, block, 0.0) for t in range(FOLD)], 0)
            high, low = split(masked)
            both = dot(high, col)
            cols = col.shape[1] // 2
            wide = both[:, :cols] + (both[:, cols:] + dot(low, col[:, :cols]))
            for q in range(2):
                chan = (2 * (d % 2) + q) * 8 + d // 2
                mine = jnp.concatenate(
                    [wide[q * PART : (q + 1) * PART], wide[(2 + q) * PART : (3 + q) * PART]], 0
                )
                high, low = split(mine)
                held[chan, :RANK, :] = high
                held[chan, RANK : 2 * RANK, :] = high
                held[chan, 2 * RANK :, :] = low

    chans = out_ref.shape[0]
    row = row_ref[...]
    for c in range(chans):
        field = dot(row, held[step * chans + c])
        out_ref[c] = (field + local_ref[c]).astype(BF16)


def expand(blocks, local, row_basis, col_basis, scale):
    chans, rows, cols = local.shape
    col = np.concatenate(halves(np.tile(col_basis.T * scale, (FOLD, 1))), 1)
    row_hi, row_lo = halves(row_basis)
    row = np.concatenate([row_hi, row_lo, row_hi], 1)
    each = 4
    grid_spec = pl.BlockSpec((each, rows, cols), lambda s: (s, 0, 0))
    whole = lambda shape: pl.BlockSpec(shape, lambda s: (0,) * len(shape))
    return pl.pallas_call(
        expand_kernel,
        grid=(chans // each,),
        in_specs=[whole(blocks.shape), grid_spec, whole(col.shape), whole(row.shape)],
        out_specs=grid_spec,
        out_shape=jax.ShapeDtypeStruct(local.shape, BF16),
        scratch_shapes=[pltpu.VMEM((chans, 3 * RANK, cols), BF16)],
        compiler_params=pltpu.CompilerParams(vmem_limit_bytes=32 * 2**20),
        name="expand",
    )(blocks, local, jnp.asarray(col), jnp.asarray(row))


def mode_work(mode_grad, spectrum, spectral_weight):
    mode_count = mode_grad.shape[0]
    chans = mode_grad.shape[2]
    weights = spectral_weight.reshape(mode_count, 2, chans, chans)
    weight_real, weight_imag = (weights[:, 0], weights[:, 1])
    grad_real, grad_imag = (mode_grad[:, 0], mode_grad[:, 1])
    saved_real, saved_imag = (spectrum[:, 0], spectrum[:, 1])
    out_real = (
        saved_real[:, :, None] * grad_real[:, None, :]
        + saved_imag[:, :, None] * grad_imag[:, None, :]
    )
    out_imag = (
        saved_real[:, :, None] * grad_imag[:, None, :]
        - saved_imag[:, :, None] * grad_real[:, None, :]
    )
    weight_grad = jnp.stack([out_real, out_imag], axis=1).reshape(mode_count, 2, chans * chans)
    back_real = jnp.sum(
        weight_real * grad_real[:, None, :] + weight_imag * grad_imag[:, None, :], axis=-1
    )
    back_imag = jnp.sum(
        weight_real * grad_imag[:, None, :] - weight_imag * grad_real[:, None, :], axis=-1
    )
    return (weight_grad, jnp.stack([back_real, back_imag], axis=1))


def on_device(cotangent, preact, spectrum, spectral_weight, point_weight):
    chans, rows_here, cols_here = cotangent.shape
    gx, gy = lax.axis_size("gx"), lax.axis_size("gy")
    grid_rows, grid_cols = rows_here * gx, cols_here * gy
    share = chans // gy
    half = K1 * K2 // (gx * gy)
    wave_rows = np.arange(K1)
    row_freqs = np.where(wave_rows < K1 // 2, wave_rows, wave_rows - K1)
    row_basis, row_waves = band_tables(row_freqs, K1 / 2 / grid_rows, grid_rows, gx)
    col_basis, col_waves = band_tables(np.arange(K2), (K2 - 1) / grid_cols, grid_cols, gy)
    col = np.stack([col_waves.real, col_waves.imag], 1).transpose(0, 3, 1, 2)
    col = col.reshape(gy * RANK, 2 * K2)
    row = np.concatenate(
        [
            np.concatenate([row_waves.real, -row_waves.imag], 2),
            np.concatenate([row_waves.imag, row_waves.real], 2),
        ],
        1,
    )
    here = lax.axis_index("gx")
    col_out = tuple(jnp.asarray(t) for t in halves(col * (1.0 / math.sqrt(K1 * K2))))
    col_back = tuple(jnp.asarray(t) for t in halves(col.T))
    row_out = tuple(jnp.asarray(t)[here] for t in halves(row))
    row_back = tuple(jnp.asarray(t)[here] for t in halves(row.transpose(0, 2, 1)))

    small = project(cotangent, preact, row_basis, col_basis)
    upstream = cotangent.astype(F32) * gelu_slope(preact.astype(F32))
    pointwise = jnp.einsum("io,oxy->ixy", point_weight, upstream, precision=lax.Precision.HIGH)

    blocks = lax.all_to_all(small, "gy", 0, 0)
    terms = to_waves(blocks, col_out, row_out).reshape(gx * gy, 2, share * half)
    got = lax.all_to_all(terms, ("gx", "gy"), 0, 0)
    got = jnp.sum(got.reshape(gx, gy, 2, share * half), axis=0).reshape(8, 2, 2, 2, half)
    mode_grad = got.transpose(4, 2, 1, 3, 0).reshape(half, 2, chans)

    weight_grad, spectrum_grad = mode_work(mode_grad, spectrum, spectral_weight)

    back = spectrum_grad.reshape(half, 2, 2, 2, 8).transpose(4, 2, 1, 3, 0)
    back = jnp.broadcast_to(back.reshape(1, gy, 2, share * half), (gx, gy, 2, share * half))
    modes = lax.all_to_all(back.reshape(gx * gy, 2, share * half), ("gx", "gy"), 0, 0)
    small = to_blocks(modes.reshape(K1, 2, 2, LANES), col_back, row_back)
    blocks = lax.all_to_all(small, "gy", 0, 0)
    scale = 1.0 / math.sqrt(grid_rows * grid_cols)
    return (expand(blocks, pointwise, row_basis, col_basis, scale), weight_grad)


def solution(mesh):
    placed = (
        P(None, "gx", "gy"),
        P(None, "gx", "gy"),
        P(("gx", "gy"), None, None),
        P(("gx", "gy"), None, None),
        P(),
    )
    return jax.shard_map(
        on_device,
        mesh=mesh,
        in_specs=placed,
        out_specs=(P(None, "gx", "gy"), P(("gx", "gy"), None, None)),
        check_vma=False,
    )
```

```python
import functools
import math

import jax
import jax.numpy as jnp
import ml_dtypes
import numpy as np
from jax import lax
from jax.experimental import pallas as pl
from jax.experimental.pallas import tpu as pltpu
from jax.sharding import PartitionSpec as P

K1 = 128
K2 = 128
RANK = 32
PART = 16
LANES = 128
FOLD = 4
GRANT = 60 * 2**20
ROWS = 32
EACH = 4

F32 = jnp.float32
BF16 = jnp.bfloat16


def slepian(length, half_band, count):
    place = np.arange(length)
    main = ((length - 1 - 2 * place) / 2.0) ** 2 * math.cos(2.0 * math.pi * half_band)
    side = place[1:] * (length - place[1:]) / 2.0
    _, vectors = np.linalg.eigh(np.diag(main) + np.diag(side, 1) + np.diag(side, -1))
    basis = vectors[:, ::-1][:, :count]
    tilt = 1.0 + (place - (length - 1) / 2.0) / length
    return basis * np.sign(np.sum(basis * tilt[:, None], axis=0))


def band_tables(freqs, half_band, grid, blocks):
    here = grid // blocks
    basis = slepian(here, half_band, RANK)
    turns = freqs[:, None] * np.arange(grid)[None, :] % grid
    waves = np.exp(-2j * math.pi * turns / grid).reshape(len(freqs), blocks, here)
    return basis, np.einsum("fbp,pn->bfn", waves, basis)


def halves(table):
    table = np.asarray(table, np.float32)
    high = table.astype(ml_dtypes.bfloat16)
    return high, (table - high.astype(np.float32)).astype(ml_dtypes.bfloat16)


def split(values):
    high = values.astype(BF16)
    return high, (values - high.astype(F32)).astype(BF16)


def dot(left, right):
    return jnp.dot(left, right, preferred_element_type=F32)


def dot3(left, right):
    return dot(left[0], right[0]) + (dot(left[0], right[1]) + dot(left[1], right[0]))


def gelu_slope(values):
    cumul = 0.5 * (1.0 + lax.erf(values * 0.7071067811865476))
    return cumul + values * jnp.exp(-0.5 * values * values) * 0.3989422804014327


def lane_group(rows):
    return lax.broadcasted_iota(jnp.int32, (rows, LANES), 1) // RANK


def low_lanes(rows):
    return lax.broadcasted_iota(jnp.int32, (rows, LANES), 1) < LANES // 2


def swap_lanes(values):
    return pltpu.roll(values, LANES // 2, 1)


def turn_blocks(pieces):
    group = lane_group(pieces[0].shape[0])
    out = []
    for t in range(FOLD):
        total = None
        for s in range(FOLD):
            shift = (s - t) * RANK % LANES
            moved = pltpu.roll(pieces[s], shift, 1) if shift else pieces[s]
            total = moved if total is None else jnp.where(group == s, moved, total)
        out.append(total)
    return out


def project_kernel(
    cot_hbm, pre_hbm, col_ref, row_hi_ref, row_lo_ref, out_ref, cot_ref, pre_ref, held, sems
):
    strips = cot_hbm.shape[1] // ROWS

    def fetch(s, source, target, which):
        place = pl.ds(s * ROWS, ROWS)
        return pltpu.make_async_copy(source.at[:, place, :], target.at[:, place, :], sems.at[which, s])

    for s in range(strips):
        fetch(s, cot_hbm, cot_ref, 0).start()
        fetch(s, pre_hbm, pre_ref, 1).start()

    count = 8 * 16
    group = lane_group(count)
    col = col_ref[...]

    def one(step, carry):
        for s in range(strips):
            @pl.when(step == s * (ROWS // 16))
            def _():
                fetch(s, cot_hbm, cot_ref, 0).wait()
                fetch(s, pre_hbm, pre_ref, 1).wait()
        rows = pl.ds(pl.multiple_of(step * 16, 16), 16)
        grad = cot_ref[:, rows, :].astype(F32)
        upstream = grad * gelu_slope(pre_ref[:, rows, :].astype(F32))
        high, low = split(upstream.reshape(FOLD * count, upstream.shape[2]))
        both = dot(high, col)
        rest = dot(low, col[:, :LANES])
        total = None
        for q in range(FOLD):
            mine = slice(q * count, (q + 1) * count)
            narrow = both[mine, :LANES] + (both[mine, LANES:] + rest[mine])
            total = narrow if total is None else jnp.where(group == q, narrow, total)
        held[:, rows, :] = total.reshape(8, 16, LANES)
        return carry

    lax.fori_loop(0, cot_hbm.shape[1] // 16, one, 0, unroll=True)

    row = (row_hi_ref[...], row_lo_ref[...])
    low = low_lanes(PART)
    for g in range(8):
        small = dot3(row, split(held[g]))
        first, second = small[:PART], small[PART:]
        out_ref[2 * g] = jnp.where(low, first, swap_lanes(second))
        out_ref[2 * g + 1] = jnp.where(low, swap_lanes(first), second)


def project(cotangent, preact, row_basis, col_basis):
    chans, rows, cols = cotangent.shape
    col_hi, col_lo = halves(np.tile(col_basis, (1, FOLD)))
    col = np.concatenate([col_hi, col_lo], 1)
    row_hi, row_lo = halves(row_basis.T)
    far = pl.BlockSpec(memory_space=pl.ANY)
    near = pl.BlockSpec(memory_space=pltpu.VMEM)
    return pl.pallas_call(
        project_kernel,
        in_specs=[far, far, near, near, near],
        out_specs=near,
        out_shape=jax.ShapeDtypeStruct((16, PART, LANES), F32),
        scratch_shapes=[
            pltpu.VMEM(cotangent.shape, BF16),
            pltpu.VMEM(cotangent.shape, BF16),
            pltpu.VMEM((8, rows, LANES), F32),
            pltpu.SemaphoreType.DMA((2, rows // ROWS)),
        ],
        compiler_params=pltpu.CompilerParams(vmem_limit_bytes=GRANT),
        name="project",
    )(cotangent, preact, jnp.asarray(col), jnp.asarray(row_hi), jnp.asarray(row_lo))


def pointwise_kernel(cot_ref, pre_ref, map_ref, out_ref, high_ref, low_ref):
    chans, rows, cols = out_ref.shape
    many = chans * 8

    @pl.when(pl.program_id(0) == 0)
    def _():
        spread = lax.broadcasted_iota(jnp.int32, (many, chans), 0) // 8
        spread = (spread == lax.broadcasted_iota(jnp.int32, (many, chans), 1)).astype(BF16)
        same = lax.broadcasted_iota(jnp.int32, (many, many), 0) % 8
        same = same == lax.broadcasted_iota(jnp.int32, (many, many), 1) % 8
        for half, target in zip(split(map_ref[...]), (high_ref, low_ref)):
            tall = dot(spread, half).astype(BF16)
            full = lax.dot_general(tall, spread, (((1,), (1,)), ((), ())), preferred_element_type=F32)
            target[...] = jnp.where(same, full, 0.0).astype(BF16)

    weights = (high_ref[...], low_ref[...])
    for part in range(rows // 16):
        place = pl.ds(part * 16, 16)
        grad = cot_ref[:, place, :].astype(F32)
        upstream = grad * gelu_slope(pre_ref[:, place, :].astype(F32))
        for sub in range(2):
            here = upstream[:, sub * 8 : (sub + 1) * 8, :].reshape(many, cols)
            mixed = dot3(weights, split(here))
            out_ref[:, pl.ds(part * 16 + sub * 8, 8), :] = mixed.reshape(chans, 8, cols)


def pointwise_map(cotangent, preact, point_weight):
    chans, rows, cols = cotangent.shape
    grid_spec = pl.BlockSpec((chans, 2 * ROWS, cols), lambda s: (0, s, 0))
    return pl.pallas_call(
        pointwise_kernel,
        grid=(rows // (2 * ROWS),),
        in_specs=[grid_spec, grid_spec, pl.BlockSpec(point_weight.shape, lambda s: (0, 0))],
        out_specs=grid_spec,
        out_shape=jax.ShapeDtypeStruct((chans, rows, cols), F32),
        scratch_shapes=[pltpu.VMEM((chans * 8, chans * 8), BF16)] * 2,
        compiler_params=pltpu.CompilerParams(vmem_limit_bytes=GRANT),
        cost_estimate=pl.CostEstimate(flops=10**10, bytes_accessed=13 * 10**6, transcendentals=3 * 10**6),
        name="pointwise_map",
    )(cotangent, preact, point_weight)


def waves_kernel(here_ref, blocks_ref, col_hi_ref, col_lo_ref, row_hi_ref, row_lo_ref, out_ref):
    strips = [turn_blocks([blocks_ref[4 * s + t] for t in range(FOLD)]) for s in range(4)]
    small = jnp.concatenate(
        [jnp.concatenate([strips[s][t] for s in range(4)], 1) for t in range(FOLD)], 0
    )
    wide = dot3(split(small), (col_hi_ref[...], col_lo_ref[...]))
    low = low_lanes(PART)
    row = (row_hi_ref[...], row_lo_ref[...])
    for half in range(2):
        tall = []
        for ri in range(2):
            for ah in range(2):
                first = wide[(2 * ah) * PART : (2 * ah + 1) * PART, ri * LANES : (ri + 1) * LANES]
                second = wide[(2 * ah + 1) * PART : (2 * ah + 2) * PART, ri * LANES : (ri + 1) * LANES]
                if half == 0:
                    tall.append(jnp.where(low, first, swap_lanes(second)))
                else:
                    tall.append(jnp.where(low, swap_lanes(first), second))
        terms = dot3(row, split(jnp.concatenate(tall, 0)))
        out_ref[:, half, 0, :] = terms[:K1]
        out_ref[:, half, 1, :] = terms[K1:]


def table_call(kernel, here, array, col, row, out_shape, name):
    whole = lambda shape: pl.BlockSpec(shape, lambda s, here: (0,) * len(shape))
    mine = pl.BlockSpec((None,) + row[0].shape[1:], lambda s, here: (here[0], 0, 0))
    return pl.pallas_call(
        kernel,
        grid_spec=pltpu.PrefetchScalarGridSpec(
            num_scalar_prefetch=1,
            grid=(1,),
            in_specs=[whole(array.shape), whole(col[0].shape), whole(col[1].shape), mine, mine],
            out_specs=whole(out_shape),
        ),
        out_shape=jax.ShapeDtypeStruct(out_shape, F32),
        name=name,
    )(here, array, *col, *row)


def to_waves(here, blocks, col, row):
    return table_call(waves_kernel, here, blocks, col, row, (K1, 2, 2, LANES), "to_waves")


def blocks_kernel(here_ref, modes_ref, col_hi_ref, col_lo_ref, row_hi_ref, row_lo_ref, out_ref):
    row = (row_hi_ref[...], row_lo_ref[...])
    tall = []
    for half in range(2):
        modes = jnp.concatenate([modes_ref[:, half, 0, :], modes_ref[:, half, 1, :]], 0)
        tall.append(dot3(row, split(modes)))
    low = low_lanes(PART)
    rows = []
    for ah in range(2):
        for q in range(2):
            cells = []
            for ri in range(2):
                place = slice(ri * RANK + ah * PART, ri * RANK + (ah + 1) * PART)
                first, second = tall[0][place], tall[1][place]
                if q == 0:
                    cells.append(jnp.where(low, first, swap_lanes(second)))
                else:
                    cells.append(jnp.where(low, swap_lanes(first), second))
            rows.append(jnp.concatenate(cells, 1))
    small = dot3(split(jnp.concatenate(rows, 0)), (col_hi_ref[...], col_lo_ref[...]))
    for s in range(4):
        pieces = turn_blocks(
            [small[t * PART : (t + 1) * PART, s * LANES : (s + 1) * LANES] for t in range(FOLD)]
        )
        for t in range(FOLD):
            out_ref[4 * s + t] = pieces[t]


def to_blocks(here, modes, col, row):
    return table_call(blocks_kernel, here, modes, col, row, (16, PART, LANES), "to_blocks")


def expand_kernel(blocks_ref, local_hbm, col_ref, row_ref, out_hbm, held, local_ref, out_ref, sems):
    chans, _, cols = out_ref.shape
    strips = chans // EACH

    def move(s, source, target, which):
        place = pl.ds(s * EACH, EACH)
        return pltpu.make_async_copy(source.at[place], target.at[place], sems.at[which, s])

    for s in range(strips):
        move(s, local_hbm, local_ref, 0).start()

    group = lane_group(PART)
    col = col_ref[...]
    for d in range(16):
        block = blocks_ref[d]
        masked = jnp.concatenate([jnp.where(group == t, block, 0.0) for t in range(FOLD)], 0)
        high, low = split(masked)
        both = dot(high, col)
        wide = both[:, :cols] + (both[:, cols:] + dot(low, col[:, :cols]))
        for q in range(2):
            chan = (2 * (d % 2) + q) * 8 + d // 2
            mine = jnp.concatenate(
                [wide[q * PART : (q + 1) * PART], wide[(2 + q) * PART : (3 + q) * PART]], 0
            )
            high, low = split(mine)
            held[chan, :RANK, :] = high
            held[chan, RANK : 2 * RANK, :] = high
            held[chan, 2 * RANK :, :] = low

    row = row_ref[...]
    for s in range(strips):
        move(s, local_hbm, local_ref, 0).wait()
        for c in range(s * EACH, (s + 1) * EACH):
            out_ref[c] = (dot(row, held[c]) + local_ref[c]).astype(BF16)
        move(s, out_ref, out_hbm, 1).start()
    for s in range(strips):
        move(s, out_ref, out_hbm, 1).wait()


def expand(blocks, local, row_basis, col_basis, scale):
    chans, rows, cols = local.shape
    col = np.concatenate(halves(np.tile(col_basis.T * scale, (FOLD, 1))), 1)
    row_hi, row_lo = halves(row_basis)
    row = np.concatenate([row_hi, row_lo, row_hi], 1)
    far = pl.BlockSpec(memory_space=pl.ANY)
    near = pl.BlockSpec(memory_space=pltpu.VMEM)
    return pl.pallas_call(
        expand_kernel,
        in_specs=[near, far, near, near],
        out_specs=far,
        out_shape=jax.ShapeDtypeStruct(local.shape, BF16),
        scratch_shapes=[
            pltpu.VMEM((chans, 3 * RANK, cols), BF16),
            pltpu.VMEM(local.shape, F32),
            pltpu.VMEM(local.shape, BF16),
            pltpu.SemaphoreType.DMA((2, chans // EACH)),
        ],
        compiler_params=pltpu.CompilerParams(vmem_limit_bytes=GRANT),
        name="expand",
    )(blocks, local, jnp.asarray(col), jnp.asarray(row))


def mode_work(mode_grad, spectrum, spectral_weight):
    mode_count = mode_grad.shape[0]
    chans = mode_grad.shape[2]
    weights = spectral_weight.reshape(mode_count, 2, chans, chans)
    weight_real, weight_imag = (weights[:, 0], weights[:, 1])
    grad_real, grad_imag = (mode_grad[:, 0], mode_grad[:, 1])
    saved_real, saved_imag = (spectrum[:, 0], spectrum[:, 1])
    out_real = (
        saved_real[:, :, None] * grad_real[:, None, :]
        + saved_imag[:, :, None] * grad_imag[:, None, :]
    )
    out_imag = (
        saved_real[:, :, None] * grad_imag[:, None, :]
        - saved_imag[:, :, None] * grad_real[:, None, :]
    )
    weight_grad = jnp.stack([out_real, out_imag], axis=1).reshape(mode_count, 2, chans * chans)
    back_real = jnp.sum(
        weight_real * grad_real[:, None, :] + weight_imag * grad_imag[:, None, :], axis=-1
    )
    back_imag = jnp.sum(
        weight_real * grad_imag[:, None, :] - weight_imag * grad_real[:, None, :], axis=-1
    )
    return (weight_grad, jnp.stack([back_real, back_imag], axis=1))


def on_device(cotangent, preact, spectrum, spectral_weight, point_weight):
    chans, rows_here, cols_here = cotangent.shape
    gx, gy = lax.axis_size("gx"), lax.axis_size("gy")
    grid_rows, grid_cols = rows_here * gx, cols_here * gy
    share = chans // gy
    half = K1 * K2 // (gx * gy)
    wave_rows = np.arange(K1)
    row_freqs = np.where(wave_rows < K1 // 2, wave_rows, wave_rows - K1)
    row_basis, row_waves = band_tables(row_freqs, K1 / 2 / grid_rows, grid_rows, gx)
    col_basis, col_waves = band_tables(np.arange(K2), (K2 - 1) / grid_cols, grid_cols, gy)
    col = np.stack([col_waves.real, col_waves.imag], 1).transpose(0, 3, 1, 2)
    col = col.reshape(gy * RANK, 2 * K2)
    row = np.concatenate(
        [
            np.concatenate([row_waves.real, -row_waves.imag], 2),
            np.concatenate([row_waves.imag, row_waves.real], 2),
        ],
        1,
    )
    here = lax.axis_index("gx").reshape(1)
    col_out = tuple(jnp.asarray(t) for t in halves(col * (1.0 / math.sqrt(K1 * K2))))
    col_back = tuple(jnp.asarray(t) for t in halves(col.T))
    row_out = tuple(jnp.asarray(t) for t in halves(row))
    row_back = tuple(jnp.asarray(t) for t in halves(row.transpose(0, 2, 1)))

    small = project(cotangent, preact, row_basis, col_basis)
    pointwise = pointwise_map(cotangent, preact, point_weight)

    blocks = lax.all_to_all(small, "gy", 0, 0)
    terms = to_waves(here, blocks, col_out, row_out).reshape(gx * gy, 2, share * half)
    got = lax.all_to_all(terms, ("gx", "gy"), 0, 0)
    got = jnp.sum(got.reshape(gx, gy, 2, share * half), axis=0).reshape(8, 2, 2, 2, half)
    mode_grad = got.transpose(4, 2, 1, 3, 0).reshape(half, 2, chans)

    weight_grad, spectrum_grad = mode_work(mode_grad, spectrum, spectral_weight)

    back = spectrum_grad.reshape(half, 2, 2, 2, 8).transpose(4, 2, 1, 3, 0)
    back = jnp.broadcast_to(back.reshape(1, gy, 2, share * half), (gx, gy, 2, share * half))
    modes = lax.all_to_all(back.reshape(gx * gy, 2, share * half), ("gx", "gy"), 0, 0)
    small = to_blocks(here, modes.reshape(K1, 2, 2, LANES), col_back, row_back)
    blocks = lax.all_to_all(small, "gy", 0, 0)
    scale = 1.0 / math.sqrt(grid_rows * grid_cols)
    return (expand(blocks, pointwise, row_basis, col_basis, scale), weight_grad)


def solution(mesh):
    placed = (
        P(None, "gx", "gy"),
        P(None, "gx", "gy"),
        P(("gx", "gy"), None, None),
        P(("gx", "gy"), None, None),
        P(),
    )
    return jax.shard_map(
        on_device,
        mesh=mesh,
        in_specs=placed,
        out_specs=(P(None, "gx", "gy"), P(("gx", "gy"), None, None)),
        check_vma=False,
    )
```

```python
import functools
import math

import jax
import jax.numpy as jnp
import ml_dtypes
import numpy as np
from jax import lax
from jax.experimental import pallas as pl
from jax.experimental.pallas import tpu as pltpu
from jax.sharding import PartitionSpec as P

K1 = 128
K2 = 128
RANK = 32
LANES = 128
FOLD = 4
GRANT = 60 * 2**20
AHEAD = 3
ROWS = (16, 32, 48, 48, 48)
STRIP = 64
EACH = 4

F32 = jnp.float32
BF16 = jnp.bfloat16


def slepian(length, half_band, count):
    place = np.arange(length)
    main = ((length - 1 - 2 * place) / 2.0) ** 2 * math.cos(2.0 * math.pi * half_band)
    side = place[1:] * (length - place[1:]) / 2.0
    _, vectors = np.linalg.eigh(np.diag(main) + np.diag(side, 1) + np.diag(side, -1))
    basis = vectors[:, ::-1][:, :count]
    tilt = 1.0 + (place - (length - 1) / 2.0) / length
    return basis * np.sign(np.sum(basis * tilt[:, None], axis=0))


def band_tables(freqs, half_band, grid, blocks):
    here = grid // blocks
    basis = slepian(here, half_band, RANK)
    turns = freqs[:, None] * np.arange(grid)[None, :] % grid
    waves = np.exp(-2j * math.pi * turns / grid).reshape(len(freqs), blocks, here)
    return basis, np.einsum("fbp,pn->bfn", waves, basis)


def halves(table):
    table = np.asarray(table, np.float32)
    high = table.astype(ml_dtypes.bfloat16)
    return high, (table - high.astype(np.float32)).astype(ml_dtypes.bfloat16)


def split(values):
    high = values.astype(BF16)
    return high, (values - high.astype(F32)).astype(BF16)


def dot(left, right):
    return jnp.dot(left, right, preferred_element_type=F32)


def dot3(left, right):
    return dot(left[0], right[0]) + (dot(left[0], right[1]) + dot(left[1], right[0]))


def gelu_slope(values):
    cumul = 0.5 * (1.0 + lax.erf(values * 0.7071067811865476))
    return cumul + values * jnp.exp(-0.5 * values * values) * 0.3989422804014327


def lane_group(rows):
    return lax.broadcasted_iota(jnp.int32, (rows, LANES), 1) // RANK


def low_lanes(rows):
    return lax.broadcasted_iota(jnp.int32, (rows, LANES), 1) < LANES // 2


def swap_lanes(values):
    return pltpu.roll(values, LANES // 2, 1)


def turn_blocks(pieces):
    group = lane_group(pieces[0].shape[0])
    out = []
    for t in range(FOLD):
        total = None
        for s in range(FOLD):
            shift = (s - t) * RANK % LANES
            moved = pltpu.roll(pieces[s], shift, 1) if shift else pieces[s]
            total = moved if total is None else jnp.where(group == s, moved, total)
        out.append(total)
    return out


def project_kernel(
    cot_hbm, pre_hbm, col_hbm, row_hbm, out_ref, cot_ref, pre_ref, held, col_ref, row_ref, sems
):
    strips = len(ROWS)
    tables = [
        pltpu.make_async_copy(source, target, sems.at[which, strips])
        for which, (source, target) in enumerate([(col_hbm, col_ref), (row_hbm, row_ref)])
    ]

    def fetch(s, source, target, which):
        place = pl.ds(sum(ROWS[:s]), ROWS[s])
        return pltpu.make_async_copy(source.at[:, place, :], target.at[:, place, :], sems.at[which, s])

    def begin(s):
        fetch(s, cot_hbm, cot_ref, 0).start()
        fetch(s, pre_hbm, pre_ref, 1).start()

    begin(0)
    for table in tables:
        table.start()
    for s in range(1, AHEAD):
        begin(s)
    tables[0].wait()

    starts = [sum(ROWS[:s]) for s in range(strips)]
    count = 8 * 16
    group = lane_group(count)
    col = col_ref[...]

    for step in range(cot_hbm.shape[1] // 16):
        if step * 16 in starts:
            s = starts.index(step * 16)
            fetch(s, cot_hbm, cot_ref, 0).wait()
            fetch(s, pre_hbm, pre_ref, 1).wait()
            if s + AHEAD < strips:
                begin(s + AHEAD)
        rows = slice(step * 16, (step + 1) * 16)
        grad = cot_ref[:, rows, :].astype(F32)
        upstream = grad * gelu_slope(pre_ref[:, rows, :].astype(F32))
        high, low = split(upstream.reshape(FOLD * count, upstream.shape[2]))
        both = dot(high, col)
        rest = dot(low, col[:, :LANES])
        total = None
        for q in range(FOLD):
            mine = slice(q * count, (q + 1) * count)
            narrow = both[mine, :LANES] + (both[mine, LANES:] + rest[mine])
            total = narrow if total is None else jnp.where(group == q, narrow, total)
        held[:, rows, :] = total.reshape(8, 16, LANES)

    tables[1].wait()
    row = (row_ref[0], row_ref[1])
    for g in range(8):
        small = dot3(row, split(held[g]))
        out_ref[2 * g] = small
        out_ref[2 * g + 1] = small


def project(cotangent, preact, row_basis, col_basis):
    chans, rows, cols = cotangent.shape
    col_hi, col_lo = halves(np.tile(col_basis, (1, FOLD)))
    col = np.concatenate([col_hi, col_lo], 1)
    row = np.stack(halves(row_basis.T))
    far = pl.BlockSpec(memory_space=pltpu.HBM)
    return pl.pallas_call(
        project_kernel,
        in_specs=[far, far, far, far],
        out_specs=pl.BlockSpec(memory_space=pltpu.VMEM),
        out_shape=jax.ShapeDtypeStruct((16, RANK, LANES), F32),
        scratch_shapes=[
            pltpu.VMEM(cotangent.shape, BF16),
            pltpu.VMEM(cotangent.shape, BF16),
            pltpu.VMEM((8, rows, LANES), F32),
            pltpu.VMEM(col.shape, BF16),
            pltpu.VMEM(row.shape, BF16),
            pltpu.SemaphoreType.DMA((2, len(ROWS) + 1)),
        ],
        compiler_params=pltpu.CompilerParams(vmem_limit_bytes=GRANT),
        name="project",
    )(cotangent, preact, jnp.asarray(col), jnp.asarray(row))


def pointwise_kernel(cot_ref, pre_ref, map_ref, out_ref, high_ref, low_ref):
    chans, rows, cols = out_ref.shape
    many = chans * 8

    @pl.when(pl.program_id(0) == 0)
    def _():
        spread = lax.broadcasted_iota(jnp.int32, (many, chans), 0) // 8
        spread = (spread == lax.broadcasted_iota(jnp.int32, (many, chans), 1)).astype(BF16)
        same = lax.broadcasted_iota(jnp.int32, (many, many), 0) % 8
        same = same == lax.broadcasted_iota(jnp.int32, (many, many), 1) % 8
        for half, target in zip(split(map_ref[...]), (high_ref, low_ref)):
            tall = dot(spread, half).astype(BF16)
            full = lax.dot_general(tall, spread, (((1,), (1,)), ((), ())), preferred_element_type=F32)
            target[...] = jnp.where(same, full, 0.0).astype(BF16)

    weights = (high_ref[...], low_ref[...])
    for part in range(rows // 16):
        place = pl.ds(part * 16, 16)
        grad = cot_ref[:, place, :].astype(F32)
        upstream = grad * gelu_slope(pre_ref[:, place, :].astype(F32))
        for sub in range(2):
            here = upstream[:, sub * 8 : (sub + 1) * 8, :].reshape(many, cols)
            mixed = dot3(weights, split(here))
            out_ref[:, pl.ds(part * 16 + sub * 8, 8), :] = mixed.reshape(chans, 8, cols)


def pointwise_map(cotangent, preact, point_weight):
    chans, rows, cols = cotangent.shape
    grid_spec = pl.BlockSpec((chans, STRIP, cols), lambda s: (0, s, 0))
    return pl.pallas_call(
        pointwise_kernel,
        grid=(rows // STRIP,),
        in_specs=[grid_spec, grid_spec, pl.BlockSpec(point_weight.shape, lambda s: (0, 0))],
        out_specs=grid_spec,
        out_shape=jax.ShapeDtypeStruct((chans, rows, cols), F32),
        scratch_shapes=[pltpu.VMEM((chans * 8, chans * 8), BF16)] * 2,
        compiler_params=pltpu.CompilerParams(vmem_limit_bytes=GRANT),
        cost_estimate=pl.CostEstimate(flops=10**10, bytes_accessed=13 * 10**6, transcendentals=3 * 10**6),
        name="pointwise_map",
    )(cotangent, preact, point_weight)


def waves_kernel(here_ref, blocks_ref, col_hi_ref, col_lo_ref, row_hi_ref, row_lo_ref, out_ref):
    strips = [turn_blocks([blocks_ref[4 * s + t] for t in range(FOLD)]) for s in range(4)]
    small = jnp.concatenate(
        [jnp.concatenate([strips[s][q] for s in range(4)], 1) for q in range(FOLD)], 0
    )
    wide = dot3(split(small), (col_hi_ref[...], col_lo_ref[...]))
    low = low_lanes(RANK)
    pairs = []
    for h in range(2):
        first = wide[2 * h * RANK : (2 * h + 1) * RANK]
        second = wide[(2 * h + 1) * RANK : (2 * h + 2) * RANK]
        real = jnp.where(low, first, swap_lanes(second))
        imag = jnp.where(low, swap_lanes(first), second)
        pairs.append(jnp.concatenate([real, imag], 0))
    terms = dot3((row_hi_ref[...], row_lo_ref[...]), split(jnp.concatenate(pairs, 1)))
    for p in range(2):
        for h in range(2):
            out_ref[:, p, h, :] = terms[p * K1 : (p + 1) * K1, h * LANES : (h + 1) * LANES]


def table_call(kernel, here, array, col, row, out_shape, name):
    whole = lambda shape: pl.BlockSpec(shape, lambda s, here: (0,) * len(shape))
    cols = pl.BlockSpec((None,) + col[0].shape[1:], lambda s, here: (here[0], 0, 0))
    rows = pl.BlockSpec((None,) + row[0].shape[1:], lambda s, here: (here[1], 0, 0))
    return pl.pallas_call(
        kernel,
        grid_spec=pltpu.PrefetchScalarGridSpec(
            num_scalar_prefetch=1,
            grid=(1,),
            in_specs=[whole(array.shape), cols, cols, rows, rows],
            out_specs=whole(out_shape),
        ),
        out_shape=jax.ShapeDtypeStruct(out_shape, F32),
        compiler_params=pltpu.CompilerParams(vmem_limit_bytes=8 * 2**20),
        name=name,
    )(here, array, *col, *row)


def to_waves(here, blocks, col, row):
    return table_call(waves_kernel, here, blocks, col, row, (K1, 2, 2, LANES), "to_waves")


def blocks_kernel(here_ref, modes_ref, col_hi_ref, col_lo_ref, row_hi_ref, row_lo_ref, out_ref):
    modes = jnp.concatenate(
        [jnp.concatenate([modes_ref[:, p, h, :] for h in range(2)], 1) for p in range(2)], 0
    )
    tall = dot3((row_hi_ref[...], row_lo_ref[...]), split(modes))
    low = low_lanes(RANK)
    rows = []
    for h in range(2):
        real = tall[:RANK, h * LANES : (h + 1) * LANES]
        imag = tall[RANK:, h * LANES : (h + 1) * LANES]
        rows.append(jnp.where(low, real, swap_lanes(imag)))
        rows.append(jnp.where(low, swap_lanes(real), imag))
    small = dot3(split(jnp.concatenate(rows, 0)), (col_hi_ref[...], col_lo_ref[...]))
    for s in range(4):
        pieces = turn_blocks(
            [small[q * RANK : (q + 1) * RANK, s * LANES : (s + 1) * LANES] for q in range(FOLD)]
        )
        for t in range(FOLD):
            out_ref[4 * s + t] = pieces[t]


def to_blocks(here, modes, col, row):
    return table_call(blocks_kernel, here, modes, col, row, (16, RANK, LANES), "to_blocks")


def expand_kernel(blocks_ref, local_hbm, col_ref, row_ref, out_hbm, held, local_ref, out_ref, sems):
    chans, _, cols = out_ref.shape
    strips = chans // EACH

    def move(s, source, target, which):
        place = pl.ds(s * EACH, EACH)
        return pltpu.make_async_copy(source.at[place], target.at[place], sems.at[which, s])

    for s in range(strips):
        move(s, local_hbm, local_ref, 0).start()

    group = lane_group(RANK)
    col = col_ref[...]
    for g in range(8):
        block = blocks_ref[2 * g] + blocks_ref[2 * g + 1]
        masked = jnp.concatenate([jnp.where(group == q, block, 0.0) for q in range(FOLD)], 0)
        high, low = split(masked)
        both = dot(high, col)
        wide = both[:, :cols] + (both[:, cols:] + dot(low, col[:, :cols]))
        high, low = split(wide)
        for q in range(FOLD):
            chan = q * 8 + g
            mine = slice(q * RANK, (q + 1) * RANK)
            held[chan, :RANK, :] = high[mine]
            held[chan, RANK : 2 * RANK, :] = high[mine]
            held[chan, 2 * RANK :, :] = low[mine]

    row = row_ref[...]
    for s in range(strips):
        move(s, local_hbm, local_ref, 0).wait()
        for c in range(s * EACH, (s + 1) * EACH):
            out_ref[c] = (dot(row, held[c]) + local_ref[c]).astype(BF16)
        move(s, out_ref, out_hbm, 1).start()
    for s in range(strips):
        move(s, out_ref, out_hbm, 1).wait()


def expand(blocks, local, row_basis, col_basis, scale):
    chans, rows, cols = local.shape
    col = np.concatenate(halves(np.tile(col_basis.T * scale, (FOLD, 1))), 1)
    row_hi, row_lo = halves(row_basis)
    row = np.concatenate([row_hi, row_lo, row_hi], 1)
    far = pl.BlockSpec(memory_space=pl.ANY)
    near = pl.BlockSpec(memory_space=pltpu.VMEM)
    return pl.pallas_call(
        expand_kernel,
        in_specs=[near, far, near, near],
        out_specs=far,
        out_shape=jax.ShapeDtypeStruct(local.shape, BF16),
        scratch_shapes=[
            pltpu.VMEM((chans, 3 * RANK, cols), BF16),
            pltpu.VMEM(local.shape, F32),
            pltpu.VMEM(local.shape, BF16),
            pltpu.SemaphoreType.DMA((2, chans // EACH)),
        ],
        compiler_params=pltpu.CompilerParams(vmem_limit_bytes=54 * 2**20),
        name="expand",
    )(blocks, local, jnp.asarray(col), jnp.asarray(row))


def mode_work(mode_grad, spectrum, spectral_weight):
    mode_count = mode_grad.shape[0]
    chans = mode_grad.shape[2]
    weights = spectral_weight.reshape(mode_count, 2, chans, chans)
    weight_real, weight_imag = (weights[:, 0], weights[:, 1])
    grad_real, grad_imag = (mode_grad[:, 0], mode_grad[:, 1])
    saved_real, saved_imag = (spectrum[:, 0], spectrum[:, 1])
    out_real = (
        saved_real[:, :, None] * grad_real[:, None, :]
        + saved_imag[:, :, None] * grad_imag[:, None, :]
    )
    out_imag = (
        saved_real[:, :, None] * grad_imag[:, None, :]
        - saved_imag[:, :, None] * grad_real[:, None, :]
    )
    weight_grad = jnp.stack([out_real, out_imag], axis=1).reshape(mode_count, 2, chans * chans)
    back_real = jnp.sum(
        weight_real * grad_real[:, None, :] + weight_imag * grad_imag[:, None, :], axis=-1
    )
    back_imag = jnp.sum(
        weight_real * grad_imag[:, None, :] - weight_imag * grad_real[:, None, :], axis=-1
    )
    return (weight_grad, jnp.stack([back_real, back_imag], axis=1))


def on_device(cotangent, preact, spectrum, spectral_weight, point_weight):
    chans, rows_here, cols_here = cotangent.shape
    gx, gy = lax.axis_size("gx"), lax.axis_size("gy")
    grid_rows, grid_cols = rows_here * gx, cols_here * gy
    half = K1 * K2 // (gx * gy)
    wave_rows = np.arange(K1)
    row_freqs = np.where(wave_rows < K1 // 2, wave_rows, wave_rows - K1)
    row_basis, row_waves = band_tables(row_freqs, K1 / 2 / grid_rows, grid_rows, gx)
    col_basis, col_waves = band_tables(np.arange(K2), (K2 - 1) / grid_cols, grid_cols, gy)
    col = np.stack([col_waves.real, col_waves.imag], 1).reshape(gy, 2, 2, half, RANK)
    col = col.transpose(2, 0, 4, 1, 3).reshape(2, gy * RANK, 2 * half)
    row = np.concatenate(
        [
            np.concatenate([row_waves.real, -row_waves.imag], 2),
            np.concatenate([row_waves.imag, row_waves.real], 2),
        ],
        1,
    )
    here = jnp.stack([lax.axis_index("gy") % 2, lax.axis_index("gx")])
    sides = [list(range(side, gx * gy, 2)) for side in range(2)]
    mates = gx * gy // 2
    col_out = tuple(jnp.asarray(t) for t in halves(col * (1.0 / math.sqrt(K1 * K2))))
    col_back = tuple(jnp.asarray(t) for t in halves(col.transpose(0, 2, 1)))
    row_out = tuple(jnp.asarray(t) for t in halves(row))
    row_back = tuple(jnp.asarray(t) for t in halves(row.transpose(0, 2, 1)))

    small = project(cotangent, preact, row_basis, col_basis)
    pointwise = pointwise_map(cotangent, preact, point_weight)

    blocks = lax.all_to_all(small, "gy", 0, 0)
    terms = to_waves(here, blocks, col_out, row_out).reshape(mates, 4, LANES)
    got = lax.all_to_all(terms, ("gx", "gy"), 0, 0, axis_index_groups=sides, tiled=True)
    got = jnp.sum(got.reshape(gx, gy // 2, 4, LANES), axis=0).reshape(8, 2, 2, 2, half)
    mode_grad = got.transpose(4, 1, 2, 3, 0).reshape(half, 2, chans)

    weight_grad, spectrum_grad = mode_work(mode_grad, spectrum, spectral_weight)

    back = spectrum_grad.reshape(half, 2, 2, 2, 8).transpose(4, 1, 2, 3, 0)
    back = jnp.broadcast_to(back.reshape(1, gy // 2, 4, LANES), (gx, gy // 2, 4, LANES))
    back = back.reshape(mates, 4, LANES)
    modes = lax.all_to_all(back, ("gx", "gy"), 0, 0, axis_index_groups=sides, tiled=True)
    small = to_blocks(here, modes.reshape(K1, 2, 2, LANES), col_back, row_back)
    blocks = lax.all_to_all(small, "gy", 0, 0)
    scale = 1.0 / math.sqrt(grid_rows * grid_cols)
    return (expand(blocks, pointwise, row_basis, col_basis, scale), weight_grad)


def solution(mesh):
    placed = (
        P(None, "gx", "gy"),
        P(None, "gx", "gy"),
        P(("gx", "gy"), None, None),
        P(("gx", "gy"), None, None),
        P(),
    )
    return jax.shard_map(
        on_device,
        mesh=mesh,
        in_specs=placed,
        out_specs=(P(None, "gx", "gy"), P(("gx", "gy"), None, None)),
        check_vma=False,
    )
```

```python
import functools
import math

import jax
import jax.numpy as jnp
import ml_dtypes
import numpy as np
from jax import lax
from jax.experimental import pallas as pl
from jax.experimental.pallas import tpu as pltpu
from jax.sharding import PartitionSpec as P

K1 = 128
K2 = 128
RANK = 32
PART = 16
LANES = 128
FOLD = 4
GRANT = 60 * 2**20
AHEAD = 3
ROWS = (16, 32, 48, 48, 48)
STRIP = 64
EACH = 4

F32 = jnp.float32
BF16 = jnp.bfloat16


def slepian(length, half_band, count):
    place = np.arange(length)
    main = ((length - 1 - 2 * place) / 2.0) ** 2 * math.cos(2.0 * math.pi * half_band)
    side = place[1:] * (length - place[1:]) / 2.0
    _, vectors = np.linalg.eigh(np.diag(main) + np.diag(side, 1) + np.diag(side, -1))
    basis = vectors[:, ::-1][:, :count]
    tilt = 1.0 + (place - (length - 1) / 2.0) / length
    return basis * np.sign(np.sum(basis * tilt[:, None], axis=0))


def band_tables(freqs, half_band, grid, blocks):
    here = grid // blocks
    basis = slepian(here, half_band, RANK)
    turns = freqs[:, None] * np.arange(grid)[None, :] % grid
    waves = np.exp(-2j * math.pi * turns / grid).reshape(len(freqs), blocks, here)
    return basis, np.einsum("fbp,pn->bfn", waves, basis)


def halves(table):
    table = np.asarray(table, np.float32)
    high = table.astype(ml_dtypes.bfloat16)
    return high, (table - high.astype(np.float32)).astype(ml_dtypes.bfloat16)


def split(values):
    high = values.astype(BF16)
    return high, (values - high.astype(F32)).astype(BF16)


def dot(left, right):
    return jnp.dot(left, right, preferred_element_type=F32)


def dot3(left, right):
    return dot(left[0], right[0]) + (dot(left[0], right[1]) + dot(left[1], right[0]))


def gelu_slope(values):
    cumul = 0.5 * (1.0 + lax.erf(values * 0.7071067811865476))
    return cumul + values * jnp.exp(-0.5 * values * values) * 0.3989422804014327


def lane_group(rows):
    return lax.broadcasted_iota(jnp.int32, (rows, LANES), 1) // RANK


def low_lanes(rows):
    return lax.broadcasted_iota(jnp.int32, (rows, LANES), 1) < LANES // 2


def swap_lanes(values):
    return pltpu.roll(values, LANES // 2, 1)


def turn_blocks(pieces):
    group = lane_group(pieces[0].shape[0])
    out = []
    for t in range(FOLD):
        total = None
        for s in range(FOLD):
            shift = (s - t) * RANK % LANES
            moved = pltpu.roll(pieces[s], shift, 1) if shift else pieces[s]
            total = moved if total is None else jnp.where(group == s, moved, total)
        out.append(total)
    return out


def project_kernel(
    cot_hbm, pre_hbm, col_hbm, row_hbm, out_ref, cot_ref, pre_ref, held, col_ref, row_ref, sems
):
    strips = len(ROWS)
    tables = [
        pltpu.make_async_copy(source, target, sems.at[which, strips])
        for which, (source, target) in enumerate([(col_hbm, col_ref), (row_hbm, row_ref)])
    ]

    def fetch(s, source, target, which):
        place = pl.ds(sum(ROWS[:s]), ROWS[s])
        return pltpu.make_async_copy(source.at[:, place, :], target.at[:, place, :], sems.at[which, s])

    def begin(s):
        fetch(s, cot_hbm, cot_ref, 0).start()
        fetch(s, pre_hbm, pre_ref, 1).start()

    begin(0)
    for table in tables:
        table.start()
    for s in range(1, AHEAD):
        begin(s)
    tables[0].wait()

    starts = [sum(ROWS[:s]) for s in range(strips)]
    count = 8 * 16
    group = lane_group(count)
    col = col_ref[...]

    for step in range(cot_hbm.shape[1] // 16):
        if step * 16 in starts:
            s = starts.index(step * 16)
            fetch(s, cot_hbm, cot_ref, 0).wait()
            fetch(s, pre_hbm, pre_ref, 1).wait()
            if s + AHEAD < strips:
                begin(s + AHEAD)
        rows = slice(step * 16, (step + 1) * 16)
        grad = cot_ref[:, rows, :].astype(F32)
        upstream = grad * gelu_slope(pre_ref[:, rows, :].astype(F32))
        high, low = split(upstream.reshape(FOLD * count, upstream.shape[2]))
        both = dot(high, col)
        rest = dot(low, col[:, :LANES])
        total = None
        for q in range(FOLD):
            mine = slice(q * count, (q + 1) * count)
            narrow = both[mine, :LANES] + (both[mine, LANES:] + rest[mine])
            total = narrow if total is None else jnp.where(group == q, narrow, total)
        held[:, rows, :] = total.reshape(8, 16, LANES)

    tables[1].wait()
    row = (row_ref[0], row_ref[1])
    low = low_lanes(PART)
    for g in range(8):
        small = dot3(row, split(held[g]))
        first, second = small[:PART], small[PART:]
        out_ref[2 * g] = jnp.where(low, first, swap_lanes(second))
        out_ref[2 * g + 1] = jnp.where(low, swap_lanes(first), second)


def project(cotangent, preact, row_basis, col_basis):
    chans, rows, cols = cotangent.shape
    col_hi, col_lo = halves(np.tile(col_basis, (1, FOLD)))
    col = np.concatenate([col_hi, col_lo], 1)
    row = np.stack(halves(row_basis.T))
    far = pl.BlockSpec(memory_space=pltpu.HBM)
    return pl.pallas_call(
        project_kernel,
        in_specs=[far, far, far, far],
        out_specs=pl.BlockSpec(memory_space=pltpu.VMEM),
        out_shape=jax.ShapeDtypeStruct((16, PART, LANES), F32),
        scratch_shapes=[
            pltpu.VMEM(cotangent.shape, BF16),
            pltpu.VMEM(cotangent.shape, BF16),
            pltpu.VMEM((8, rows, LANES), F32),
            pltpu.VMEM(col.shape, BF16),
            pltpu.VMEM(row.shape, BF16),
            pltpu.SemaphoreType.DMA((2, len(ROWS) + 1)),
        ],
        compiler_params=pltpu.CompilerParams(vmem_limit_bytes=GRANT),
        name="project",
    )(cotangent, preact, jnp.asarray(col), jnp.asarray(row))


def pointwise_kernel(cot_ref, pre_ref, map_ref, out_ref, high_ref, low_ref):
    chans, rows, cols = out_ref.shape
    many = chans * 8

    @pl.when(pl.program_id(0) == 0)
    def _():
        spread = lax.broadcasted_iota(jnp.int32, (many, chans), 0) // 8
        spread = (spread == lax.broadcasted_iota(jnp.int32, (many, chans), 1)).astype(BF16)
        same = lax.broadcasted_iota(jnp.int32, (many, many), 0) % 8
        same = same == lax.broadcasted_iota(jnp.int32, (many, many), 1) % 8
        for half, target in zip(split(map_ref[...]), (high_ref, low_ref)):
            tall = dot(spread, half).astype(BF16)
            full = lax.dot_general(tall, spread, (((1,), (1,)), ((), ())), preferred_element_type=F32)
            target[...] = jnp.where(same, full, 0.0).astype(BF16)

    weights = (high_ref[...], low_ref[...])
    for part in range(rows // 16):
        place = pl.ds(part * 16, 16)
        grad = cot_ref[:, place, :].astype(F32)
        upstream = grad * gelu_slope(pre_ref[:, place, :].astype(F32))
        for sub in range(2):
            here = upstream[:, sub * 8 : (sub + 1) * 8, :].reshape(many, cols)
            mixed = dot3(weights, split(here))
            out_ref[:, pl.ds(part * 16 + sub * 8, 8), :] = mixed.reshape(chans, 8, cols)


def pointwise_map(cotangent, preact, point_weight):
    chans, rows, cols = cotangent.shape
    grid_spec = pl.BlockSpec((chans, STRIP, cols), lambda s: (0, s, 0))
    return pl.pallas_call(
        pointwise_kernel,
        grid=(rows // STRIP,),
        in_specs=[grid_spec, grid_spec, pl.BlockSpec(point_weight.shape, lambda s: (0, 0))],
        out_specs=grid_spec,
        out_shape=jax.ShapeDtypeStruct((chans, rows, cols), F32),
        scratch_shapes=[pltpu.VMEM((chans * 8, chans * 8), BF16)] * 2,
        compiler_params=pltpu.CompilerParams(vmem_limit_bytes=GRANT),
        cost_estimate=pl.CostEstimate(flops=10**10, bytes_accessed=13 * 10**6, transcendentals=3 * 10**6),
        name="pointwise_map",
    )(cotangent, preact, point_weight)


def waves_kernel(here_ref, blocks_ref, col_hi_ref, col_lo_ref, row_hi_ref, row_lo_ref, out_ref):
    strips = [turn_blocks([blocks_ref[4 * s + t] for t in range(FOLD)]) for s in range(4)]
    small = jnp.concatenate(
        [jnp.concatenate([strips[s][t] for s in range(4)], 1) for t in range(FOLD)], 0
    )
    wide = dot3(split(small), (col_hi_ref[...], col_lo_ref[...]))
    low = low_lanes(PART)
    row = (row_hi_ref[...], row_lo_ref[...])
    for half in range(2):
        tall = []
        for ri in range(2):
            for ah in range(2):
                first = wide[(2 * ah) * PART : (2 * ah + 1) * PART, ri * LANES : (ri + 1) * LANES]
                second = wide[(2 * ah + 1) * PART : (2 * ah + 2) * PART, ri * LANES : (ri + 1) * LANES]
                if half == 0:
                    tall.append(jnp.where(low, first, swap_lanes(second)))
                else:
                    tall.append(jnp.where(low, swap_lanes(first), second))
        terms = dot3(row, split(jnp.concatenate(tall, 0)))
        out_ref[:, half, 0, :] = terms[:K1]
        out_ref[:, half, 1, :] = terms[K1:]


def table_call(kernel, here, array, col, row, out_shape, name):
    whole = lambda shape: pl.BlockSpec(shape, lambda s, here: (0,) * len(shape))
    mine = pl.BlockSpec((None,) + row[0].shape[1:], lambda s, here: (here[0], 0, 0))
    return pl.pallas_call(
        kernel,
        grid_spec=pltpu.PrefetchScalarGridSpec(
            num_scalar_prefetch=1,
            grid=(1,),
            in_specs=[whole(array.shape), whole(col[0].shape), whole(col[1].shape), mine, mine],
            out_specs=whole(out_shape),
        ),
        out_shape=jax.ShapeDtypeStruct(out_shape, F32),
        compiler_params=pltpu.CompilerParams(vmem_limit_bytes=8 * 2**20),
        name=name,
    )(here, array, *col, *row)


def to_waves(here, blocks, col, row):
    return table_call(waves_kernel, here, blocks, col, row, (K1, 2, 2, LANES), "to_waves")


def blocks_kernel(here_ref, modes_ref, col_hi_ref, col_lo_ref, row_hi_ref, row_lo_ref, out_ref):
    row = (row_hi_ref[...], row_lo_ref[...])
    tall = []
    for half in range(2):
        modes = jnp.concatenate([modes_ref[:, half, 0, :], modes_ref[:, half, 1, :]], 0)
        tall.append(dot3(row, split(modes)))
    low = low_lanes(PART)
    rows = []
    for ah in range(2):
        for q in range(2):
            cells = []
            for ri in range(2):
                place = slice(ri * RANK + ah * PART, ri * RANK + (ah + 1) * PART)
                first, second = tall[0][place], tall[1][place]
                if q == 0:
                    cells.append(jnp.where(low, first, swap_lanes(second)))
                else:
                    cells.append(jnp.where(low, swap_lanes(first), second))
            rows.append(jnp.concatenate(cells, 1))
    small = dot3(split(jnp.concatenate(rows, 0)), (col_hi_ref[...], col_lo_ref[...]))
    for s in range(4):
        pieces = turn_blocks(
            [small[t * PART : (t + 1) * PART, s * LANES : (s + 1) * LANES] for t in range(FOLD)]
        )
        for t in range(FOLD):
            out_ref[4 * s + t] = pieces[t]


def to_blocks(here, modes, col, row):
    return table_call(blocks_kernel, here, modes, col, row, (16, PART, LANES), "to_blocks")


def expand_kernel(blocks_ref, local_hbm, col_ref, row_ref, out_hbm, held, local_ref, out_ref, sems):
    chans, _, cols = out_ref.shape
    strips = chans // EACH

    def move(s, source, target, which):
        place = pl.ds(s * EACH, EACH)
        return pltpu.make_async_copy(source.at[place], target.at[place], sems.at[which, s])

    for s in range(strips):
        move(s, local_hbm, local_ref, 0).start()

    group = lane_group(PART)
    col = col_ref[...]
    for d in range(16):
        block = blocks_ref[d]
        masked = jnp.concatenate([jnp.where(group == t, block, 0.0) for t in range(FOLD)], 0)
        high, low = split(masked)
        both = dot(high, col)
        wide = both[:, :cols] + (both[:, cols:] + dot(low, col[:, :cols]))
        for q in range(2):
            chan = (2 * (d % 2) + q) * 8 + d // 2
            mine = jnp.concatenate(
                [wide[q * PART : (q + 1) * PART], wide[(2 + q) * PART : (3 + q) * PART]], 0
            )
            high, low = split(mine)
            held[chan, :RANK, :] = high
            held[chan, RANK : 2 * RANK, :] = high
            held[chan, 2 * RANK :, :] = low

    row = row_ref[...]
    for s in range(strips):
        move(s, local_hbm, local_ref, 0).wait()
        for c in range(s * EACH, (s + 1) * EACH):
            out_ref[c] = (dot(row, held[c]) + local_ref[c]).astype(BF16)
        move(s, out_ref, out_hbm, 1).start()
    for s in range(strips):
        move(s, out_ref, out_hbm, 1).wait()


def expand(blocks, local, row_basis, col_basis, scale):
    chans, rows, cols = local.shape
    col = np.concatenate(halves(np.tile(col_basis.T * scale, (FOLD, 1))), 1)
    row_hi, row_lo = halves(row_basis)
    row = np.concatenate([row_hi, row_lo, row_hi], 1)
    far = pl.BlockSpec(memory_space=pl.ANY)
    near = pl.BlockSpec(memory_space=pltpu.VMEM)
    return pl.pallas_call(
        expand_kernel,
        in_specs=[near, far, near, near],
        out_specs=far,
        out_shape=jax.ShapeDtypeStruct(local.shape, BF16),
        scratch_shapes=[
            pltpu.VMEM((chans, 3 * RANK, cols), BF16),
            pltpu.VMEM(local.shape, F32),
            pltpu.VMEM(local.shape, BF16),
            pltpu.SemaphoreType.DMA((2, chans // EACH)),
        ],
        compiler_params=pltpu.CompilerParams(vmem_limit_bytes=50 * 2**20),
        name="expand",
    )(blocks, local, jnp.asarray(col), jnp.asarray(row))


def mode_work(mode_grad, spectrum, spectral_weight):
    mode_count = mode_grad.shape[0]
    chans = mode_grad.shape[2]
    weights = spectral_weight.reshape(mode_count, 2, chans, chans)
    weight_real, weight_imag = (weights[:, 0], weights[:, 1])
    grad_real, grad_imag = (mode_grad[:, 0], mode_grad[:, 1])
    saved_real, saved_imag = (spectrum[:, 0], spectrum[:, 1])
    out_real = (
        saved_real[:, :, None] * grad_real[:, None, :]
        + saved_imag[:, :, None] * grad_imag[:, None, :]
    )
    out_imag = (
        saved_real[:, :, None] * grad_imag[:, None, :]
        - saved_imag[:, :, None] * grad_real[:, None, :]
    )
    weight_grad = jnp.stack([out_real, out_imag], axis=1).reshape(mode_count, 2, chans * chans)
    back_real = jnp.sum(
        weight_real * grad_real[:, None, :] + weight_imag * grad_imag[:, None, :], axis=-1
    )
    back_imag = jnp.sum(
        weight_real * grad_imag[:, None, :] - weight_imag * grad_real[:, None, :], axis=-1
    )
    return (weight_grad, jnp.stack([back_real, back_imag], axis=1))


def on_device(cotangent, preact, spectrum, spectral_weight, point_weight):
    chans, rows_here, cols_here = cotangent.shape
    gx, gy = lax.axis_size("gx"), lax.axis_size("gy")
    grid_rows, grid_cols = rows_here * gx, cols_here * gy
    share = chans // gy
    half = K1 * K2 // (gx * gy)
    wave_rows = np.arange(K1)
    row_freqs = np.where(wave_rows < K1 // 2, wave_rows, wave_rows - K1)
    row_basis, row_waves = band_tables(row_freqs, K1 / 2 / grid_rows, grid_rows, gx)
    col_basis, col_waves = band_tables(np.arange(K2), (K2 - 1) / grid_cols, grid_cols, gy)
    col = np.stack([col_waves.real, col_waves.imag], 1).transpose(0, 3, 1, 2)
    col = col.reshape(gy * RANK, 2 * K2)
    row = np.concatenate(
        [
            np.concatenate([row_waves.real, -row_waves.imag], 2),
            np.concatenate([row_waves.imag, row_waves.real], 2),
        ],
        1,
    )
    here = lax.axis_index("gx").reshape(1)
    col_out = tuple(jnp.asarray(t) for t in halves(col * (1.0 / math.sqrt(K1 * K2))))
    col_back = tuple(jnp.asarray(t) for t in halves(col.T))
    row_out = tuple(jnp.asarray(t) for t in halves(row))
    row_back = tuple(jnp.asarray(t) for t in halves(row.transpose(0, 2, 1)))

    small = project(cotangent, preact, row_basis, col_basis)
    pointwise = pointwise_map(cotangent, preact, point_weight)

    blocks = lax.all_to_all(small, "gy", 0, 0)
    terms = to_waves(here, blocks, col_out, row_out).reshape(gx * gy, 2, share * half)
    got = lax.all_to_all(terms, ("gx", "gy"), 0, 0)
    got = jnp.sum(got.reshape(gx, gy, 2, share * half), axis=0).reshape(8, 2, 2, 2, half)
    mode_grad = got.transpose(4, 2, 1, 3, 0).reshape(half, 2, chans)

    weight_grad, spectrum_grad = mode_work(mode_grad, spectrum, spectral_weight)

    back = spectrum_grad.reshape(half, 2, 2, 2, 8).transpose(4, 2, 1, 3, 0)
    back = jnp.broadcast_to(back.reshape(1, gy, 2, share * half), (gx, gy, 2, share * half))
    modes = lax.all_to_all(back.reshape(gx * gy, 2, share * half), ("gx", "gy"), 0, 0)
    small = to_blocks(here, modes.reshape(K1, 2, 2, LANES), col_back, row_back)
    blocks = lax.all_to_all(small, "gy", 0, 0)
    scale = 1.0 / math.sqrt(grid_rows * grid_cols)
    return (expand(blocks, pointwise, row_basis, col_basis, scale), weight_grad)


def solution(mesh):
    placed = (
        P(None, "gx", "gy"),
        P(None, "gx", "gy"),
        P(("gx", "gy"), None, None),
        P(("gx", "gy"), None, None),
        P(),
    )
    return jax.shard_map(
        on_device,
        mesh=mesh,
        in_specs=placed,
        out_specs=(P(None, "gx", "gy"), P(("gx", "gy"), None, None)),
        check_vma=False,
    )
```
